512 devices in a mesh: dp: 16 (over z_hi, y), ctx: 32 (over x, z_lo, core).
Axes of the slice: x: 4, y: 8, z: 8 (z_hi: 2, z_lo: 4; z = z_hi * 4 + z_lo), core: 2. Of those that a mesh axis runs over, the one named last changes fastest.
Arguments:
- queries: bfloat16 [65536, 4096], P(('dp', 'ctx')), may hold values from -6 to 6
- keys: bfloat16 [65536, 512], P(('dp', 'ctx')), may hold values from -6 to 6
- values: bfloat16 [65536, 512], P(('dp', 'ctx')), may hold values from -6 to 6
- out_grad: bfloat16 [65536, 4096], P(('dp', 'ctx')), may hold values from -6 to 6
- inputs: bfloat16 [65536, 5120], P(('dp', 'ctx')), may hold values from -24 to 24
- permutation: int32 [16, 64], P('dp'), may hold values from 0 to 63, each once within a row
- lengths: int32 [16, 4], P('dp'), may hold values from 1 to 2048, 4096 in all within a row
Outputs:
- query_grad: bfloat16 [65536, 4096], P(('dp', 'ctx'))
- kv_grad: bfloat16 [65536, 1024], P(('dp', 'ctx'))
- weight_grad: float32 [5120, 1024], P(('dp', 'ctx'))
The draws below stay inside these ranges and needn't reach their ends.
Inputs may be any that keep to these rules, and one draw needn't show every extreme that they name: `lengths`: each row sums to 4096; its largest entry is 2048.
All inputs are finite; a program needn't handle non-finite values.
Results may differ from the reference program's by a relative error of at most 0.011.
Values may be sent and summed in bfloat16 or wider, within the bound.
A program may use at most 64 MiB of HBM per device.

```python
import math
import jax
import jax.numpy as jnp
import numpy as np
from jax import lax

D = 5120
HQ = 32
GKV = 4
DH = 128
SPAN = 64
NSEG = 4
HG = 8
SEQ = 4096
MOST = 2048
TOKENS = 65536
N_DP = 16
N_CTX = 32


def draw_queries(key, part):
    key = jax.random.fold_in(key, 11)
    base = jnp.clip(jax.random.normal(key, (TOKENS, GKV, HG, DH), jnp.float32), -6.0, 6.0)
    return base.reshape(TOKENS, HQ * DH).astype(jnp.bfloat16)


def draw_keys(key, part):
    key = jax.random.fold_in(key, 23)
    base = jnp.clip(jax.random.normal(key, (TOKENS, GKV, DH), jnp.float32), -6.0, 6.0)
    return base.reshape(TOKENS, GKV * DH).astype(jnp.bfloat16)


def with_spikes(values, key, source, target, shards_of, factor):
    def block_of(position):
        return (jnp.arange(values.shape[position]) // (values.shape[position] // shards_of)).reshape((-1,) + (1,) * (values.ndim - 1 - position))

    first = jax.random.permutation(key, shards_of)[block_of(target)]
    far = (block_of(target) + shards_of // 2) % shards_of
    return jnp.where((block_of(source) == first) | (block_of(source) == far), factor * values, values)


def level_of(rng, shape, split, low, top_value):
    level = 1.0
    for axis_at, parts in split:
        steps = jax.random.uniform(jax.random.fold_in(jax.random.fold_in(rng, 6), axis_at), (parts,), jnp.float32, low / len(split), top_value / len(split))
        level = level * jnp.repeat(jnp.exp(steps), shape[axis_at] // parts).reshape((-1,) + (1,) * (len(shape) - 1 - axis_at))
    return level


def length_profile(amount, total, reach, skew):
    portions = [(1 << 20) // math.isqrt(grade ** skew) + 1 for grade in range(2, amount + 1)]
    spare, holding = total - reach - (amount - 1), [1] * (amount - 1)
    while spare > 0:
        movable = [i for i in range(amount - 1) if holding[i] < reach]
        pool, budget = sum([portions[i] for i in movable]), spare
        for i in movable:
            extra = min(reach - holding[i], max(1, budget * portions[i] // pool), spare)
            holding[i] = holding[i] + extra
            spare = spare - extra
    return np.array([reach] + holding)


def uneven(key, amount, total, most, slope):
    if amount == 2:
        one = jax.random.randint(key, (), max(1, total - most), min(most, total - 1) + 1)
        return jnp.stack([one, total - one])
    tallies = jnp.asarray(length_profile(amount, total, most, slope), jnp.int32)
    pairs = (amount - 1) // 2
    source_of, sink = tallies[1:1 + 2 * pairs:2], tallies[2:2 + 2 * pairs:2]
    margin = jnp.minimum(source_of - 1, most - sink)
    passed = jax.random.randint(jax.random.fold_in(key, 1), (pairs,), 0, 1 << 20) % (margin + 1)
    tallies = tallies.at[1:1 + 2 * pairs:2].set(source_of - passed).at[2:2 + 2 * pairs:2].set(sink + passed)
    return tallies[jax.random.permutation(jax.random.fold_in(key, 2), amount)]


def normal_values(rng, shape, scale, bound, shards=(), kind=jnp.bfloat16):
    factor_of = level_of(rng, shape, shards, -0.22, 0.18) if shards else 1.0
    values = jax.random.normal(rng, shape, jnp.float32) * scale * factor_of
    return jnp.minimum(jnp.maximum(values, -bound), bound).astype(kind)


def gaussian_with(key, extent, scale, bound, pieces, heavy, held_as=jnp.bfloat16):
    values = scale * jax.random.normal(key, extent, jnp.float32)
    if pieces:
        values = values * level_of(key, extent, pieces, -0.22, 0.18)
    return jnp.clip(with_spikes(values, jax.random.fold_in(key, 3), *heavy), -bound, bound).astype(held_as)


def setup_inputs(seed: int = 0) -> dict:
    arg_keys = jax.random.split(jax.random.key(seed), 8)
    queries = draw_queries(jax.random.fold_in(arg_keys[7], 71), 0)
    keys = draw_keys(jax.random.fold_in(arg_keys[7], 71), 0)
    values = normal_values(arg_keys[2], (TOKENS, GKV * DH), 1.0, 6.0, ((0, 512),))
    out_grad = normal_values(arg_keys[3], (TOKENS, HQ * DH), 1.0, 6.0, ((0, 512),))
    inputs = gaussian_with(arg_keys[4], (TOKENS, D), 1.0, 24.0, ((0, 512),), (0, 1, 512, 6.0))
    permutation = jax.vmap(lambda own: jax.random.permutation(own, 2 * N_CTX))(jax.random.split(arg_keys[5], N_DP)).reshape((N_DP, 2 * N_CTX)).astype(jnp.int32)
    lengths = jax.vmap(lambda own: uneven(own, NSEG, SEQ, MOST, 2))(jax.random.split(arg_keys[6], N_DP)).reshape((N_DP, NSEG)).astype(jnp.int32)
    return dict(queries=queries, keys=keys, values=values, out_grad=out_grad, inputs=inputs, permutation=permutation, lengths=lengths)


def shard_grads(query_rows, key_rows, value_rows, grad_rows, query_pos, key_pos, query_seg, key_seg):
    rows = query_rows.shape[0]
    width = key_rows.shape[0]
    scale = 1.0 / (DH ** 0.5)
    qf = query_rows.astype(jnp.float32).reshape(rows, GKV, HG, DH)
    kf = key_rows.astype(jnp.float32).reshape(width, GKV, DH)
    vf = value_rows.astype(jnp.float32).reshape(width, GKV, DH)
    gf = grad_rows.astype(jnp.float32).reshape(rows, GKV, HG, DH)
    allowed = (key_pos[None, :] <= query_pos[:, None]) & (key_seg[None, :] == query_seg[:, None])
    score = jnp.einsum('rgqd,kgd->gqrk', qf, kf) * scale
    masked = jnp.where(allowed, score, -1e30)
    top = jnp.max(masked, axis=-1, keepdims=True)
    expo = jnp.where(allowed, jnp.exp(masked - top), 0.0)
    prob = expo / jnp.sum(expo, axis=-1, keepdims=True)
    prob_low = prob.astype(jnp.bfloat16)
    prob_low = lax.optimization_barrier(prob_low).astype(jnp.float32)
    output = jnp.einsum('gqrk,kgd->rgqd', prob_low, vf)
    delta = jnp.sum(gf * output, axis=-1)
    dprob = jnp.einsum('rgqd,kgd->gqrk', gf, vf)
    dscore = prob * (dprob - jnp.transpose(delta, (1, 2, 0))[..., None])
    dscore = lax.optimization_barrier(dscore.astype(jnp.bfloat16)).astype(jnp.float32)
    query_grad = (jnp.einsum('gqrk,kgd->rgqd', dscore, kf) * scale).astype(jnp.bfloat16)
    key_part = jnp.einsum('gqrk,rgqd->kgd', dscore, qf) * scale
    value_part = jnp.einsum('gqrk,rgqd->kgd', prob_low, gf)
    return (query_grad.reshape(rows, HQ * DH), key_part.reshape(width, GKV * DH),
            value_part.reshape(width, GKV * DH))


def reference(queries, keys, values, out_grad, inputs, permutation, lengths):
    rows = 2 * SPAN

    def one_group(group):
        start = (group * SEQ).astype(jnp.int32)

        def take(array):
            return lax.dynamic_slice_in_dim(array, start, SEQ, 0).reshape(N_CTX, rows, array.shape[1])

        qs, ks, vs, gs = take(queries), take(keys), take(values), take(out_grad)
        order = permutation[group]
        bounds = jnp.cumsum(lengths[group])[:-1]
        offsets = jnp.arange(SPAN, dtype=jnp.int32)
        pos = (order.reshape(N_CTX, 2)[:, :, None] * SPAN + offsets[None, None, :]).reshape(N_CTX, rows)
        seg = jnp.sum((pos[..., None] >= bounds[None, None, :]).astype(jnp.int32), axis=-1)

        def one_shard(shard):
            prior = (shard + N_CTX - 1) % N_CTX
            key_rows = jnp.concatenate([ks[prior], ks[shard]], axis=0)
            value_rows = jnp.concatenate([vs[prior], vs[shard]], axis=0)
            key_pos = jnp.concatenate([pos[prior], pos[shard]], axis=0)
            key_seg = jnp.concatenate([seg[prior], seg[shard]], axis=0)
            return shard_grads(qs[shard], key_rows, value_rows, gs[shard], pos[shard], key_pos, seg[shard], key_seg)

        query_grad, key_part, value_part = lax.map(one_shard, jnp.arange(N_CTX, dtype=jnp.int32))
        key_total = key_part[:, rows:] + jnp.roll(key_part[:, :rows], -1, axis=0)
        value_total = value_part[:, rows:] + jnp.roll(value_part[:, :rows], -1, axis=0)
        kv_grad = jnp.concatenate([key_total.reshape(SEQ, GKV * DH), value_total.reshape(SEQ, GKV * DH)], axis=1)
        return query_grad.reshape(SEQ, HQ * DH), kv_grad.astype(jnp.bfloat16)

    query_grad, kv_grad = lax.map(one_group, jnp.arange(N_DP, dtype=jnp.int32))
    query_grad = query_grad.reshape(TOKENS, HQ * DH)
    kv_grad = kv_grad.reshape(TOKENS, 2 * GKV * DH)
    weight_grad = jnp.dot(inputs.T, kv_grad, preferred_element_type=jnp.float32)
    return query_grad, kv_grad, weight_grad
```

```python
import functools
import math

import jax
import jax.numpy as jnp
from jax import lax
from jax.experimental import pallas as pl
from jax.experimental.pallas import tpu as pltpu
from jax.sharding import PartitionSpec as P

DH = 128
NZH, NY, NX, NZL, NC = 2, 8, 4, 4, 2
NZ = NZH * NZL
PAIR = 2
PAD = 16
MESH = pl.DeviceIdType.MESH
F32, BF16 = jnp.float32, jnp.bfloat16
NT = (((1,), (1,)), ((), ()))
NN = (((1,), (0,)), ((), ()))
TN = (((0,), (0,)), ((), ()))


def dot(a, b, dims):
    return lax.dot_general(a, b, dims, preferred_element_type=F32)


def kernel(
    order, lens, q_hbm, k_hbm, v_hbm, og_hbm, x_hbm, qg_out, kv_out, w_out,
    x_v, q_v, og_v, kall, vall, bias, qg_v, acc, back, brecv, kvg, gbuf, xt, xr,
    ys, yr, pf, zf, zs, zr, ry, rz, s2y, r2y, s2z, r2z,
    loc, kvo_sem, kv_s, kv_r, x_s, x_r, f_s, f_r, b_s, b_r, g_s, g_r,
    ys_s, ys_r, zs_s, zs_r, y2_s, y2_r, z2_s, z2_r,
):
    rows = k_hbm.shape[0]
    span = rows // 2
    heads = k_hbm.shape[1] // DH
    shared = q_hbm.shape[1] // (DH * heads)
    chunks = heads // PAIR
    width = PAIR * DH
    own = w_out.shape[0]
    octet = NZL * NC * own
    scale = 1.0 / DH**0.5

    dp, ctx = lax.axis_index("dp"), lax.axis_index("ctx")
    cycle = NX * NZL * NC
    zhi, y = dp // NY, dp % NY
    x, zlo, core = ctx // (NZL * NC), (ctx // NC) % NZL, ctx % NC
    z = zhi * NZL + zlo
    after, before = (ctx + 1) % cycle, (ctx + cycle - 1) % cycle

    def at_x(d, e):
        return (dp, ((x + d) % NX) * (NZL * NC) + zlo * NC + (core + e) % NC)

    def at_y(d, e):
        return (zhi * NY + (y + d) % NY, x * (NZL * NC) + zlo * NC + (core + e) % NC)

    def at_z(d, e):
        to = (z + d) % NZ
        return ((to // NZL) * NY + y, x * (NZL * NC) + (to % NZL) * NC + (core + e) % NC)

    def remote(src, dst, send, recv, to):
        return pltpu.make_async_remote_copy(
            src_ref=src, dst_ref=dst, send_sem=send, recv_sem=recv, device_id=to, device_id_type=MESH
        )

    load_x = pltpu.make_async_copy(x_hbm, x_v, loc.at[0])
    load_k = pltpu.make_async_copy(k_hbm, kall.at[pl.ds(rows, rows)], loc.at[1])
    load_v = pltpu.make_async_copy(v_hbm, vall.at[pl.ds(rows, rows)], loc.at[2])
    load_q = pltpu.make_async_copy(q_hbm, q_v, loc.at[3])
    load_og = pltpu.make_async_copy(og_hbm, og_v, loc.at[4])
    for load in (load_x, load_k, load_v, load_q, load_og):
        load.start()

    partners = [(dp, after), (dp, before)]
    partners += [at_x(d, e) for d in range(NX) for e in range(NC) if d or e]
    partners += [at_y(d, e) for d in range(1, NY) for e in range(NC)]
    partners += [at_z(d, e) for d in range(1, NZ) for e in range(NC)]
    barrier = pltpu.get_barrier_semaphore()
    for to in partners:
        pl.semaphore_signal(barrier, inc=1, device_id=to, device_id_type=MESH)
    pl.semaphore_wait(barrier, len(partners))

    kv_copies = [
        remote(k_hbm, kall.at[pl.ds(0, rows)], kv_s.at[0], kv_r.at[0], (dp, after)),
        remote(v_hbm, vall.at[pl.ds(0, rows)], kv_s.at[1], kv_r.at[1], (dp, after)),
    ]
    for copy in kv_copies:
        copy.start()

    load_x.wait()
    two = 2 * NX * octet
    for i in range(NZH * NY // 2):
        turned = jnp.transpose(x_v[:, i * two : (i + 1) * two])
        xt[2 * i : 2 * i + 2] = turned.reshape(2, NX, octet, rows)
    x_copies = []
    for d in (2, 1, 3) if NX == 4 else range(1, NX):
        copy = remote(
            xt.at[:, (x + d) % NX], xr.at[:, :, pl.ds(d * rows, rows)],
            x_s.at[d], x_r.at[d], at_x(d, 0),
        )
        copy.start()
        x_copies.append(copy)
    own_x = pltpu.make_async_copy(xt.at[:, x], xr.at[:, :, pl.ds(0, rows)], loc.at[5])
    own_x.start()

    prior = (ctx + cycle - 1) % cycle
    key_slots = [order[0, 2 * prior], order[0, 2 * prior + 1], order[0, 2 * ctx], order[0, 2 * ctx + 1]]
    bounds = [lens[0, 0]]
    for i in range(1, lens.shape[1] - 1):
        bounds.append(bounds[-1] + lens[0, i])

    def rank(pos):
        seg = jnp.zeros(pos.shape, jnp.int32)
        for bound in bounds:
            seg = seg + (pos >= bound).astype(jnp.int32)
        return seg

    shape = (2 * rows, rows)
    key_at = lax.broadcasted_iota(jnp.int32, shape, 0)
    query_at = lax.broadcasted_iota(jnp.int32, shape, 1)
    key_slot = jnp.where(
        key_at < rows,
        jnp.where(key_at < span, key_slots[0], key_slots[1]),
        jnp.where(key_at < rows + span, key_slots[2], key_slots[3]),
    )
    query_slot = jnp.where(query_at < span, key_slots[2], key_slots[3])
    key_pos = key_slot * span + key_at % span
    query_pos = query_slot * span + query_at % span
    allowed = (key_pos <= query_pos) & (rank(key_pos) == rank(query_pos))
    term = jnp.where(allowed, 0.0, -1e30).astype(F32)
    bias[:, :rows] = term
    bias[:, rows:] = term

    own_x.wait()
    hand_own = remote(
        xr.at[:, :, pl.ds(0, rows)], xr.at[:, :, pl.ds(NX * rows, rows)], f_s.at[0], f_r.at[0], at_x(0, 1)
    )
    hand_own.start()
    hands = [hand_own]

    load_k.wait()
    load_v.wait()
    load_q.wait()
    load_og.wait()
    for copy in kv_copies:
        copy.wait_recv()

    def attend(c):
        def one_head(i, carry):
            head = c * PAIR + i
            lanes = pl.ds(pl.multiple_of(head * DH, DH), DH)
            keys, values = kall[:, lanes], vall[:, lanes]
            key_sum = value_sum = None
            for p in range(shared // 2):
                first = (head * shared + 2 * p) * DH
                cols = [pl.ds(pl.multiple_of(first + j * DH, DH), DH) for j in range(2)]
                query = jnp.concatenate([q_v[:, cols[0]], q_v[:, cols[1]]], axis=0)
                grad = jnp.concatenate([og_v[:, cols[0]], og_v[:, cols[1]]], axis=0)
                score = dot(keys, query, NT) + bias[...]
                top = jnp.max(score, axis=0, keepdims=True)
                expo = jnp.exp2((score - top) * (scale * math.log2(math.e)))
                prob = expo * (1.0 / jnp.sum(expo, axis=0, keepdims=True))
                prob_low = prob.astype(BF16)
                dprob = dot(values, grad, NT)
                delta = jnp.sum(prob_low.astype(F32) * dprob, axis=0, keepdims=True)
                dscore = (prob * (dprob - delta)).astype(BF16)
                query_grad = (dot(dscore, keys, TN) * scale).astype(BF16)
                qg_v[:, cols[0]] = query_grad[:rows]
                qg_v[:, cols[1]] = query_grad[rows:]
                key_term = dot(dscore, query, NN)
                value_term = dot(prob_low, grad, NN)
                key_sum = key_term if p == 0 else key_sum + key_term
                value_sum = value_term if p == 0 else value_sum + value_term
            key_sum = key_sum * scale
            spot = pl.ds(pl.multiple_of(i * DH, DH), DH)
            acc[c, 0, :, spot] = key_sum[rows:]
            acc[c, 1, :, spot] = value_sum[rows:]
            back[c, 0, :, spot] = key_sum[:rows].astype(BF16)
            back[c, 1, :, spot] = value_sum[:rows].astype(BF16)
            return carry

        lax.fori_loop(0, PAIR, one_head, 0)

    back_copies, out_copies = [], []
    for c in range(chunks):
        attend(c)
        copy = remote(back.at[c], brecv.at[c], b_s.at[c], b_r.at[c], (dp, before))
        copy.start()
        back_copies.append(copy)
        wide = PAIR * shared * DH
        cols = pl.ds(c * wide, wide)
        copy = pltpu.make_async_copy(qg_v.at[:, cols], qg_out.at[:, cols], kvo_sem.at[c])
        copy.start()
        out_copies.append(copy)

    g_copies = []

    def finish(c):
        back_copies[c].wait_recv()
        for t in range(2):
            kvg[c, t] = (acc[c, t] + brecv[c, t].astype(F32)).astype(BF16)
        gbuf[c, 0] = kvg[c, core]
        copies = []
        for d in (2, 1, 3, 0) if NX == 4 else range(NX):
            for e in range(NC):
                if d or e:
                    slot = e * NX + d
                    copy = remote(
                        kvg.at[c, (core + e) % NC], gbuf.at[c, slot],
                        g_s.at[c, slot], g_r.at[c, slot], at_x(d, e),
                    )
                    copy.start()
                    copies.append(copy)
        g_copies.append(copies)
        for t in range(2):
            cols = pl.ds(t * heads * DH + c * width, width)
            copy = pltpu.make_async_copy(kvg.at[c, t], kv_out.at[:, cols], kvo_sem.at[chunks + 2 * c + t])
            copy.start()
            out_copies.append(copy)

    finish(0)

    for copy, d in zip(x_copies, (2, 1, 3) if NX == 4 else range(1, NX)):
        copy.wait_recv()
        hand = remote(
            xr.at[:, :, pl.ds(d * rows, rows)], xr.at[:, :, pl.ds((NX + d) * rows, rows)],
            f_s.at[d], f_r.at[d], at_x(0, 1),
        )
        hand.start()
        hands.append(hand)

    for c in range(1, chunks):
        finish(c)
    for hand in hands:
        hand.wait_recv()

    far_y = sorted(range(1, NY), key=lambda d: -min(d, NY - d))
    far_z = sorted(range(1, NZ), key=lambda d: -min(d, NZ - d))
    y_copies, z_copies = [], []
    piece = NC * own

    def multiply(c):
        for copy in g_copies[c]:
            copy.wait_recv()
        right = gbuf[c].reshape(NX * NC * rows, width)
        for h in range(NZH):
            left = xr[h * NY : (h + 1) * NY].reshape(NY * octet, NX * NC * rows)
            part = dot(left, right, NN)
            ys[c, h] = part[:, :DH].astype(BF16).reshape(NY, octet, DH)
            pf[...] = part[:, DH:]
            for i in range(NY):
                for j in range(NZL):
                    zf[h * NZL + j, i * piece : (i + 1) * piece] = pf[
                        i * octet + j * piece : i * octet + (j + 1) * piece
                    ]
        zs[c] = zf[...].astype(BF16)
        copies = []
        for d in far_y:
            copy = remote(
                ys.at[c, :, (y + d) % NY], yr.at[c, d - 1], ys_s.at[c, d - 1], ys_r.at[c, d - 1], at_y(d, 0)
            )
            copy.start()
            copies.append(copy)
        y_copies.append(copies)
        copies = []
        for d in far_z:
            copy = remote(
                zs.at[c, (z + d) % NZ], zr.at[c, d - 1], zs_s.at[c, d - 1], zs_r.at[c, d - 1], at_z(d, 0)
            )
            copy.start()
            copies.append(copy)
        z_copies.append(copies)

    for c in range(chunks):
        multiply(c)

    ends = []

    def second(send_from, land, send, recv, where, spot, count):
        for d in range(count):
            for e in range(NC):
                if d or e:
                    copy = remote(
                        send_from.at[spot(d), (core + e) % NC], land.at[d * NC + e], send, recv, where(d, e)
                    )
                    copy.start()
        land[0] = send_from[spot(0), core]
        ends.append((land, send, recv))

    ry[:, octet:] = jnp.zeros((NZH, ry.shape[1] - octet, DH), F32)
    rz[NY * piece :] = jnp.zeros((rz.shape[0] - NY * piece, DH), F32)

    def reduce(c):
        total = ys[c, :, y].astype(F32)
        for copy in y_copies[c]:
            copy.wait_recv()
        for d in range(NY - 1):
            total = total + yr[c, d].astype(F32)
        ry[:, :octet] = total
        for h in range(NZH):
            for j in range(NZL):
                for k in range(NC):
                    start = (j * NC + k) * own
                    s2y[c, h * NZL + j, k] = ry[h, start : start + PAD].astype(BF16)
        second(
            s2y.at[c], r2y.at[c], y2_s.at[c], y2_r.at[c], at_z, lambda d: (z + d) % NZ, NZ
        )
        total = zs[c, z].astype(F32)
        for copy in z_copies[c]:
            copy.wait_recv()
        for d in range(NZ - 1):
            total = total + zr[c, d].astype(F32)
        rz[: NY * piece] = total
        for i in range(NY):
            for k in range(NC):
                start = (i * NC + k) * own
                s2z[c, i, k] = rz[start : start + PAD].astype(BF16)
        second(
            s2z.at[c], r2z.at[c], z2_s.at[c], z2_r.at[c], at_y, lambda d: (y + d) % NY, NY
        )

    for c in range(chunks):
        reduce(c)

    for c in range(chunks):
        for kind in range(2):
            land, send, recv = ends[2 * c + kind]
            others = land.at[pl.ds(1, land.shape[0] - 1)]
            pltpu.make_async_copy(others, others, recv).wait()
            for e in range(NC):
                total = land[e].astype(F32)
                for d in range(1, land.shape[0] // NC):
                    total = total + land[d * NC + e].astype(F32)
                col = ((core + e) % NC) * heads * DH + c * width + kind * DH
                w_out[:, pl.ds(pl.multiple_of(col, DH), DH)] = total[:own]

    for copy in kv_copies + x_copies + hands + back_copies:
        copy.wait_send()
    for copies in g_copies + y_copies + z_copies:
        for copy in copies:
            copy.wait_send()
    for land, send, recv in ends:
        others = land.at[pl.ds(1, land.shape[0] - 1)]
        pltpu.make_async_copy(others, others, send).wait()
    for copy in out_copies:
        copy.wait()


def body(queries, keys, values, out_grad, inputs, permutation, lengths):
    rows, model = inputs.shape
    heads = keys.shape[1] // DH
    chunks = heads // PAIR
    width = PAIR * DH
    own = model // (NZH * NY * NX * NZL * NC)
    octet = NZL * NC * own
    piece = NC * own
    room = lambda n: -(-(n - own + PAD) // 8) * 8
    vmem = lambda shape, kind: pltpu.VMEM(shape, kind)
    dma = lambda *shape: pltpu.SemaphoreType.DMA(shape)
    scratch = [
        vmem((rows, model), BF16),
        vmem(queries.shape, BF16),
        vmem(queries.shape, BF16),
        vmem((2 * rows, heads * DH), BF16),
        vmem((2 * rows, heads * DH), BF16),
        vmem((2 * rows, 2 * rows), F32),
        vmem(queries.shape, BF16),
        vmem((chunks, 2, rows, width), F32),
        vmem((chunks, 2, rows, width), BF16),
        vmem((chunks, 2, rows, width), BF16),
        vmem((chunks, 2, rows, width), BF16),
        vmem((chunks, NX * NC, rows, width), BF16),
        vmem((NZH * NY, NX, octet, rows), BF16),
        vmem((NZH * NY, octet, NX * NC * rows), BF16),
        vmem((chunks, NZH, NY, octet, DH), BF16),
        vmem((chunks, NY - 1, NZH, octet, DH), BF16),
        vmem((NY * octet, DH), F32),
        vmem((NZ, NY * piece, DH), F32),
        vmem((chunks, NZ, NY * piece, DH), BF16),
        vmem((chunks, NZ - 1, NY * piece, DH), BF16),
        vmem((NZH, room(octet), DH), F32),
        vmem((room(NY * piece), DH), F32),
        vmem((chunks, NZ, NC, PAD, DH), BF16),
        vmem((chunks, NZ * NC, PAD, DH), BF16),
        vmem((chunks, NY, NC, PAD, DH), BF16),
        vmem((chunks, NY * NC, PAD, DH), BF16),
        dma(6), dma(3 * chunks),
        dma(2), dma(2),
        dma(NX), dma(NX), dma(NX), dma(NX),
        dma(chunks), dma(chunks),
        dma(chunks, NX * NC), dma(chunks, NX * NC),
        dma(chunks, NY - 1), dma(chunks, NY - 1),
        dma(chunks, NZ - 1), dma(chunks, NZ - 1),
        dma(chunks), dma(chunks), dma(chunks), dma(chunks),
    ]
    smem = pl.BlockSpec(memory_space=pltpu.SMEM)
    anywhere = pl.BlockSpec(memory_space=pl.ANY)
    return pl.pallas_call(
        kernel,
        out_shape=(
            jax.ShapeDtypeStruct(queries.shape, BF16),
            jax.ShapeDtypeStruct((rows, 2 * heads * DH), BF16),
            jax.ShapeDtypeStruct((own, 2 * heads * DH), F32),
        ),
        in_specs=[smem, smem] + [anywhere] * 5,
        out_specs=(anywhere, anywhere, pl.BlockSpec(memory_space=pltpu.VMEM)),
        scratch_shapes=scratch,
        compiler_params=pltpu.CompilerParams(
            collective_id=0, has_side_effects=True, vmem_limit_bytes=48 * 1024 * 1024
        ),
    )(permutation, lengths, queries, keys, values, out_grad, inputs)


def solution(mesh):
    both = P(("dp", "ctx"), None)
    return jax.shard_map(
        body,
        mesh=mesh,
        in_specs=(both, both, both, both, both, P("dp", None), P("dp", None)),
        out_specs=(both, both, both),
        check_vma=False,
    )
```

```python
import functools
import math

import jax
import jax.numpy as jnp
from jax import lax
from jax.experimental import pallas as pl
from jax.experimental.pallas import tpu as pltpu
from jax.sharding import PartitionSpec as P

DH = 128
NZH, NY, NX, NZL, NC = 2, 8, 4, 4, 2
NZ = NZH * NZL
PAD = 16
FAR = (4, 3, 5, 2, 6, 1, 7)
RELAYED = ()
MESH = pl.DeviceIdType.MESH
F32, BF16 = jnp.float32, jnp.bfloat16
NT = (((1,), (1,)), ((), ()))
NN = (((1,), (0,)), ((), ()))
TN = (((0,), (0,)), ((), ()))


def dot(a, b, dims):
    return lax.dot_general(a, b, dims, preferred_element_type=F32)


def kernel(
    order_hbm, lens_hbm, q_hbm, k_hbm, v_hbm, og_hbm, x_hbm, qg_out, kv_out, w_out,
    order, lens, x_v, qo_v, kv_v, bias, qg_v, acc, back, brecv, kvg, gbuf, xt, xr,
    pf, zf, sent, got, tt, mm, s2, r2, wv,
    loc, out_sem, kv_s, kv_r, x_s, x_r, hand_s, hand_r, b_s, b_r, g_s, g_r, one_s, one_r, two_s, two_r,
):
    rows = k_hbm.shape[0]
    span = rows // 2
    heads = k_hbm.shape[1] // DH
    shared = q_hbm.shape[1] // (DH * heads)
    own = w_out.shape[0]
    octet = NZL * NC * own
    piece = NC * own
    scale = 1.0 / DH**0.5

    dp, ctx = lax.axis_index("dp"), lax.axis_index("ctx")
    cycle = NX * NZL * NC
    zhi, y = dp // NY, dp % NY
    x, zlo, core = ctx // (NZL * NC), (ctx // NC) % NZL, ctx % NC
    z = zhi * NZL + zlo
    after, before = (ctx + 1) % cycle, (ctx + cycle - 1) % cycle

    def device(x, y, z, e):
        return ((z // NZL) * NY + y, x * (NZL * NC) + (z % NZL) * NC + (core + e) % NC)

    def in_x(d, e):
        return device((x + d) % NX, y, z, e)

    def in_y(d, e):
        return device(x, (y + d) % NY, z, e)

    def in_z(d, e):
        return device(x, y, (z + d) % NZ, e)

    rings = ((y, in_y), (z, in_z))

    def spot(kind, d):
        return (rings[kind][0] + d) % NZ

    def remote(src, dst, send, recv, to):
        copy = pltpu.make_async_remote_copy(
            src_ref=src, dst_ref=dst, send_sem=send, recv_sem=recv, device_id=to, device_id_type=MESH
        )
        copy.start()

    def wait(array, sem):
        pltpu.make_async_copy(array, array, sem).wait()

    partners = [(dp, after), (dp, before)]
    partners += [in_x(d, e) for d in range(NX) for e in range(NC) if d or e]
    partners += [where(d, e) for _, where in rings for d in range(1, NZ) for e in range(NC)]
    barrier = pltpu.get_barrier_semaphore()
    load_x = pltpu.make_async_copy(x_hbm, x_v, loc.at[0])
    load_x.start()
    for to in partners:
        pl.semaphore_signal(barrier, inc=1, device_id=to, device_id_type=MESH)

    here = pl.ds(rows, rows)
    load_order = pltpu.make_async_copy(order_hbm, order, loc.at[1])
    load_lens = pltpu.make_async_copy(lens_hbm, lens, loc.at[2])
    load_order.start()
    load_lens.start()
    for i, array in enumerate((k_hbm, v_hbm)):
        pltpu.make_async_copy(array, kv_v.at[i, here], loc.at[3]).start()
    for i, array in enumerate((q_hbm, og_hbm)):
        pltpu.make_async_copy(array, qo_v.at[i], loc.at[4]).start()

    load_x.wait()
    two = 2 * NX * octet
    with jax.named_scope("turn"):
        for i in range(NZH * NY // 2):
            turned = jnp.transpose(x_v[:, i * two : (i + 1) * two])
            xt[2 * i : 2 * i + 2] = turned.reshape(2, NX, octet, rows)

    with jax.named_scope("barrier_wait"):
        pl.semaphore_wait(barrier, len(partners))

    there = pl.ds(0, rows)

    def head_cols(c):
        return pl.ds(c * DH, DH)

    for c in range(heads):
        for i, src in enumerate((k_hbm, v_hbm)):
            remote(src.at[:, head_cols(c)], kv_v.at[i, there, head_cols(c)], kv_s.at[0], kv_r.at[c], (dp, after))

    def slots(d, count=1, e=0):
        return pl.ds((e * NX + d) * rows, count * rows)

    for d in (2, 3, 1):
        remote(xt.at[:, (x + d) % NX], xr.at[:, :, slots(d)], x_s.at[0], x_r.at[d], in_x(d, 0))
    own_x = pltpu.make_async_copy(xt.at[:, x], xr.at[:, :, slots(0)], loc.at[5])
    own_x.start()

    load_order.wait()
    load_lens.wait()
    prior = (ctx + cycle - 1) % cycle
    key_slots = [order[0, 2 * prior], order[0, 2 * prior + 1], order[0, 2 * ctx], order[0, 2 * ctx + 1]]
    bounds = [lens[0, 0]]
    for i in range(1, lens.shape[1] - 1):
        bounds.append(bounds[-1] + lens[0, i])

    def rank(pos):
        seg = jnp.zeros(pos.shape, jnp.int32)
        for bound in bounds:
            seg = seg + (pos >= bound).astype(jnp.int32)
        return seg

    shape = (2 * rows, rows)
    key_at = lax.broadcasted_iota(jnp.int32, shape, 0)
    query_at = lax.broadcasted_iota(jnp.int32, shape, 1)
    key_slot = jnp.where(
        key_at < rows,
        jnp.where(key_at < span, key_slots[0], key_slots[1]),
        jnp.where(key_at < rows + span, key_slots[2], key_slots[3]),
    )
    query_slot = jnp.where(query_at < span, key_slots[2], key_slots[3])
    key_pos = key_slot * span + key_at % span
    query_pos = query_slot * span + query_at % span
    allowed = (key_pos <= query_pos) & (rank(key_pos) == rank(query_pos))
    term = jnp.where(allowed, 0.0, -1e30).astype(F32)
    bias[...] = term

    own_x.wait()

    def hand(d):
        remote(xr.at[:, :, slots(d)], xr.at[:, :, slots(d, 1, 1)], hand_s.at[0], hand_r.at[0], in_x(0, 1))

    hand(0)
    wait(kv_v.at[:, here], loc.at[3])
    wait(qo_v, loc.at[4])

    def attend(c):
        keys, values = kv_v[0, :, head_cols(c)], kv_v[1, :, head_cols(c)]
        cols = [head_cols(c * shared + j) for j in range(shared)]
        query = jnp.concatenate([qo_v[0, :, col] for col in cols], axis=0)
        grad = jnp.concatenate([qo_v[1, :, col] for col in cols], axis=0)
        score = dot(keys, query, NT) + jnp.concatenate([bias[...]] * shared, axis=1)
        dprob = dot(values, grad, NT)
        top = jnp.max(score, axis=0, keepdims=True)
        expo = jnp.exp2((score - top) * (scale * math.log2(math.e)))
        prob = expo * (1.0 / jnp.sum(expo, axis=0, keepdims=True))
        prob_low = prob.astype(BF16)
        delta = jnp.sum(prob_low.astype(F32) * dprob, axis=0, keepdims=True)
        dscore = (prob * (dprob - delta)).astype(BF16)
        key_sum = dot(dscore, query, NN) * scale
        value_sum = dot(prob_low, grad, NN)
        back[c, 0] = key_sum[:rows].astype(BF16)
        back[c, 1] = value_sum[:rows].astype(BF16)
        remote(back.at[c], brecv.at[c], b_s.at[0], b_r.at[c], (dp, before))
        acc[c, 0] = key_sum[rows:]
        acc[c, 1] = value_sum[rows:]
        query_grad = (dot(dscore, keys, TN) * scale).astype(BF16)
        for j, col in enumerate(cols):
            qg_v[:, col] = query_grad[j * rows : (j + 1) * rows]

    for c in range(heads):
        with jax.named_scope("kv_wait"):
            wait(kv_v.at[:, there, head_cols(c)], kv_r.at[c])
        with jax.named_scope(f"attention{c}"):
            attend(c)
        cols = pl.ds(c * shared * DH, shared * DH)
        pltpu.make_async_copy(qg_v.at[:, cols], qg_out.at[:, cols], out_sem.at[0]).start()

    def finish(c):
        with jax.named_scope("back_wait"):
            wait(brecv.at[c], b_r.at[c])
        for t in range(2):
            kvg[c, t] = (acc[c, t] + brecv[c, t].astype(F32)).astype(BF16)
        for d, e in ((2, 0), (2, 1), (1, 0), (3, 0), (1, 1), (3, 1), (0, 1)):
            if d != 2 or c not in RELAYED:
                remote(kvg.at[c, (core + e) % NC], gbuf.at[c, e * NX + d], g_s.at[0], g_r.at[c, int(d == 2)], in_x(d, e))
        gbuf[c, 0] = kvg[c, core]
        for t in range(2):
            pltpu.make_async_copy(kvg.at[c, t], kv_out.at[:, head_cols(t * heads + c)], out_sem.at[1]).start()

    with jax.named_scope("kv_grad0"):
        finish(0)
    with jax.named_scope("kv_grad1"):
        finish(1)
    with jax.named_scope("x_wait3"):
        wait(xr.at[:, :, slots(3)], x_r.at[3])
    hand(3)
    with jax.named_scope("kv_grad2"):
        finish(2)
    with jax.named_scope("kv_grad3"):
        finish(3)
    with jax.named_scope("x_wait1"):
        wait(xr.at[:, :, slots(1)], x_r.at[1])
    hand(1)
    with jax.named_scope("x_wait2"):
        wait(xr.at[:, :, slots(2)], x_r.at[2])
    hand(2)

    def send_first(c, kind):
        for d in FAR:
            remote(
                sent.at[c, kind, spot(kind, d)], got.at[c, kind, d - 1], one_s.at[0], one_r.at[c, kind],
                rings[kind][1](d, 0),
            )

    def join(one, other):
        lane = lax.broadcasted_iota(jnp.int32, one.shape, 1)
        return jnp.where(lane < DH // 2, one, other)

    def swap(value):
        return pltpu.roll(value, DH // 2, 1)

    def multiply(c):
        with jax.named_scope("g_wait"):
            if c not in RELAYED:
                wait(gbuf.at[c, pl.ds(0, NX * NC - 3)], g_r.at[c, 0])
            wait(gbuf.at[c, pl.ds(0, NC)], g_r.at[c, 1])
        parts = [
            dot(
                xr[h * NY : (h + 1) * NY].reshape(NY * octet, NX * NC * rows),
                gbuf[c].reshape(NX * NC * rows, DH), NN,
            )
            for h in range(NZH)
        ]
        sent[c, 0] = join(parts[0], swap(parts[1])).astype(BF16).reshape(NY, octet, DH)
        send_first(c, 0)
        middle = NY * octet // 2
        for h in range(NZH):
            pf[h] = join(swap(parts[h][:middle]), parts[h][middle:])
            for i in range(NY // 2):
                for j in range(NZL):
                    zf[h * NZL + j, i * piece : (i + 1) * piece] = pf[
                        h, i * octet + j * piece : i * octet + (j + 1) * piece
                    ]
        sent[c, 1] = zf[...].astype(BF16)
        send_first(c, 1)

    def reduce(c, kind):
        with jax.named_scope("last_wait"):
            wait(got.at[c, kind], one_r.at[c, kind])
        total = sent[c, kind, spot(kind, 0)].astype(F32)
        for i in range(NY - 1):
            total = total + got[c, kind, i].astype(F32)
        tt[c, kind, :octet] = total

    def second(q, kind):
        one, other = tt[2 * q, kind], tt[2 * q + 1, kind]
        mm[0] = join(one, swap(other))
        mm[1] = join(swap(one), other)
        for h in range(2):
            for k in range(NZL * NC):
                s2[q, kind, h * NZL + k // NC, k % NC] = mm[h, k * own : k * own + PAD].astype(BF16)
        for d in FAR + (0,):
            for e in range(NC):
                if d or e:
                    remote(
                        s2.at[q, kind, spot(1 - kind, d), (core + e) % NC], r2.at[q, kind, d * NC + e],
                        two_s.at[0], two_r.at[q, kind], rings[1 - kind][1](d, e),
                    )
        r2[q, kind, 0] = s2[q, kind, spot(1 - kind, 0), core]

    def total_of(q, kind):
        with jax.named_scope("second_wait"):
            wait(r2.at[q, kind, pl.ds(1, NY * NC - 1)], two_r.at[q, kind])
        sums = []
        for e in range(NC):
            total = r2[q, kind, e].astype(F32)
            for d in range(1, NY):
                total = total + r2[q, kind, d * NC + e].astype(F32)
            sums.append(total)
        return sums

    tt[:, :, octet:] = jnp.zeros((heads, 2, tt.shape[2] - octet, DH), F32)
    with jax.named_scope("hand_wait"):
        wait(xr.at[:, :, slots(0, NX, 1)], hand_r.at[0])

    def both(stage, c):
        with jax.named_scope(f"{stage.__name__}{c}"):
            stage(c, 0)
            stage(c, 1)

    with jax.named_scope("product0"):
        multiply(0)
    with jax.named_scope("product1"):
        multiply(1)
    with jax.named_scope("product2"):
        multiply(2)
    with jax.named_scope("product3"):
        multiply(3)
    both(reduce, 0)
    both(reduce, 1)
    both(second, 0)
    both(reduce, 2)
    both(reduce, 3)
    both(second, 1)

    with jax.named_scope("sends"):
        wait(kv_v.at[:, there], kv_s.at[0])
        wait(xr.at[:, :, slots(1, NX - 1)], x_s.at[0])
        wait(xr.at[:, :, slots(0, NX, 1)], hand_s.at[0])
        wait(brecv, b_s.at[0])
        wait(gbuf.at[:, pl.ds(1, NX * NC - 1)], g_s.at[0])
        wait(got, one_s.at[0])
        pltpu.make_async_copy(qg_v, qg_out, out_sem.at[0]).wait()
        wait(kv_out, out_sem.at[1])

    for q in range(heads // 2):
        one, other = total_of(q, 0), total_of(q, 1)
        for e in range(NC):
            for i, value in enumerate((join(one[e], swap(other[e])), join(swap(one[e]), other[e]))):
                col = (((core + e) % NC) * heads + 2 * q + i) * DH
                wv[:, pl.ds(pl.multiple_of(col, DH), DH)] = value[:own]
    with jax.named_scope("last"):
        copy = pltpu.make_async_copy(wv, w_out, out_sem.at[2])
        copy.start()
        wait(r2.at[:, :, pl.ds(1, NY * NC - 1)], two_s.at[0])
        copy.wait()


def place(qg_in, kv_in, w_in, qg_out, kv_out, w_out, qg, kv, w, got, put):
    rows = qg.shape[0] // 4
    plan = [(qg_in, qg_out, qg, pl.ds(i * rows, rows)) for i in range(4)]
    plan += [(kv_in, kv_out, kv, pl.ds(i * 2 * rows, 2 * rows)) for i in range(2)]
    plan += [(w_in, w_out, w, pl.ds(0, w.shape[0]))]
    loads = [pltpu.make_async_copy(a.at[r], v.at[r], got.at[i]) for i, (a, _, v, r) in enumerate(plan)]
    stores = [pltpu.make_async_copy(v.at[r], b.at[r], put.at[i]) for i, (_, b, v, r) in enumerate(plan)]
    for load in loads:
        load.start()
    for load, store in zip(loads, stores):
        load.wait()
        store.start()
    for store in stores:
        store.wait()


def body(queries, keys, values, out_grad, inputs, permutation, lengths):
    rows, model = inputs.shape
    heads = keys.shape[1] // DH
    own = model // (NZH * NY * NX * NZL * NC)
    octet = NZL * NC * own
    room = -(-(octet - own + PAD) // 8) * 8
    vmem = lambda kind, *shape: pltpu.VMEM(shape, kind)
    dma = lambda *shape: pltpu.SemaphoreType.DMA(shape)
    scratch = [
        pltpu.SMEM(permutation.shape, jnp.int32),
        pltpu.SMEM(lengths.shape, jnp.int32),
        vmem(BF16, rows, model),
        vmem(BF16, 2, *queries.shape),
        vmem(BF16, 2, 2 * rows, heads * DH),
        vmem(F32, 2 * rows, rows),
        vmem(BF16, *queries.shape),
        vmem(F32, heads, 2, rows, DH),
        vmem(BF16, heads, 2, rows, DH),
        vmem(BF16, heads, 2, rows, DH),
        vmem(BF16, heads, 2, rows, DH),
        vmem(BF16, heads, NX * NC, rows, DH),
        vmem(BF16, NZH * NY, NX, octet, rows),
        vmem(BF16, NZH * NY, octet, NX * NC * rows),
        vmem(F32, NZH, NY * octet // 2, DH),
        vmem(F32, NZ, octet, DH),
        vmem(BF16, heads, 2, NY, octet, DH),
        vmem(BF16, heads, 2, NY - 1, octet, DH),
        vmem(F32, heads, 2, room, DH),
        vmem(F32, 2, room, DH),
        vmem(BF16, heads // 2, 2, NY, NC, PAD, DH),
        vmem(BF16, heads // 2, 2, NY * NC, PAD, DH),
        vmem(F32, own, 2 * heads * DH),
        dma(6), dma(3),
        dma(1), dma(heads),
        dma(1), dma(NX), dma(1), dma(1),
        dma(1), dma(heads),
        dma(1), dma(heads, 2),
        dma(1), dma(heads, 2),
        dma(1), dma(heads // 2, 2),
    ]
    anywhere = pl.BlockSpec(memory_space=pl.ANY)
    shapes = (
        jax.ShapeDtypeStruct(queries.shape, BF16),
        jax.ShapeDtypeStruct((rows, 2 * heads * DH), BF16),
        jax.ShapeDtypeStruct((own, 2 * heads * DH), F32),
    )
    results = pl.pallas_call(
        kernel,
        out_shape=shapes,
        in_specs=[anywhere] * 7,
        out_specs=(anywhere,) * 3,
        scratch_shapes=scratch,
        compiler_params=pltpu.CompilerParams(
            collective_id=0, has_side_effects=True, vmem_limit_bytes=63 * 1024 * 1024
        ),
    )(permutation, lengths, queries, keys, values, out_grad, inputs)
    return pl.pallas_call(
        place,
        out_shape=shapes,
        in_specs=[anywhere] * 3,
        out_specs=(anywhere,) * 3,
        scratch_shapes=[vmem(r.dtype, *r.shape) for r in shapes] + [dma(7), dma(7)],
        compiler_params=pltpu.CompilerParams(vmem_limit_bytes=63 * 1024 * 1024),
    )(*results)


def solution(mesh):
    both = P(("dp", "ctx"), None)
    return jax.shard_map(
        body,
        mesh=mesh,
        in_specs=(both, both, both, both, both, P("dp", None), P("dp", None)),
        out_specs=(both, both, both),
        check_vma=False,
    )
```

```python
import functools
import math

import jax
import jax.numpy as jnp
from jax import lax
from jax.experimental import pallas as pl
from jax.experimental.pallas import tpu as pltpu
from jax.sharding import PartitionSpec as P

DH = 128
NZH, NY, NX, NZL, NC = 2, 8, 4, 4, 2
NZ = NZH * NZL
PAD = 16
FAR = (4, 3, 5, 2, 6, 1, 7)
RELAYED = ()
CUT = 48
STEPS = (0, 1, 2)
MESH = pl.DeviceIdType.MESH
F32, BF16 = jnp.float32, jnp.bfloat16
NT = (((1,), (1,)), ((), ()))
NN = (((1,), (0,)), ((), ()))
TN = (((0,), (0,)), ((), ()))


def dot(a, b, dims):
    return lax.dot_general(a, b, dims, preferred_element_type=F32)


def kernel(
    order_hbm, lens_hbm, q_hbm, k_hbm, v_hbm, og_hbm, x_hbm, qg_out, kv_out, w_out,
    order, lens, x_v, qo_v, kv_v, bias, qg_v, acc, back, brecv, kvg, gbuf, xt, xr,
    pf, zf, sent, comb, got, tt, mm, s2, r2, wv,
    loc, out_sem, kv_s, kv_r, x_s, x_r, hand_s, hand_r, b_s, b_r, g_s, g_r, one_s, one_r, two_s, two_r,
):
    rows = k_hbm.shape[0]
    span = rows // 2
    heads = k_hbm.shape[1] // DH
    shared = q_hbm.shape[1] // (DH * heads)
    own = w_out.shape[0]
    octet = NZL * NC * own
    piece = NC * own
    scale = 1.0 / DH**0.5

    dp, ctx = lax.axis_index("dp"), lax.axis_index("ctx")
    cycle = NX * NZL * NC
    zhi, y = lax.div(dp, NY), lax.rem(dp, NY)
    x, zlo, core = lax.div(ctx, NZL * NC), lax.rem(lax.div(ctx, NC), NZL), lax.rem(ctx, NC)
    z = zhi * NZL + zlo
    after, before = lax.rem(ctx + 1, cycle), lax.rem(ctx + cycle - 1, cycle)

    def device(x, y, z, e):
        return (lax.div(z, NZL) * NY + y, x * (NZL * NC) + lax.rem(z, NZL) * NC + (lax.rem(core + e, NC) if e else core))

    def in_x(d, e):
        return device(lax.rem(x + d, NX), y, z, e)

    def in_y(d, e):
        return device(x, lax.rem(y + NY + d, NY), z, e)

    def in_z(d, e):
        return device(x, y, lax.rem(z + NZ + d, NZ), e)

    rings = ((y, in_y), (z, in_z))

    def spot(kind, d):
        return lax.rem(rings[kind][0] + NZ + d, NZ)

    def remote(src, dst, send, recv, to):
        copy = pltpu.make_async_remote_copy(
            src_ref=src, dst_ref=dst, send_sem=send, recv_sem=recv, device_id=to, device_id_type=MESH
        )
        copy.start()

    def wait(array, sem):
        pltpu.make_async_copy(array, array, sem).wait()

    partners = [(dp, after), (dp, before)]
    partners += [where(d, e) for d in FAR for _, where in rings for e in range(NC)]
    partners += [in_x(d, e) for d in range(NX) for e in range(NC) if d or e]
    barrier = pltpu.get_barrier_semaphore()
    load_x = pltpu.make_async_copy(x_hbm, x_v, loc.at[0])
    load_x.start()
    for to in partners:
        pl.semaphore_signal(barrier, inc=1, device_id=to, device_id_type=MESH)

    here = pl.ds(rows, rows)
    load_order = pltpu.make_async_copy(order_hbm, order, loc.at[1])
    load_lens = pltpu.make_async_copy(lens_hbm, lens, loc.at[2])
    load_order.start()
    load_lens.start()
    for i, array in enumerate((k_hbm, v_hbm)):
        pltpu.make_async_copy(array, kv_v.at[i, here], loc.at[3]).start()
    for i, array in enumerate((q_hbm, og_hbm)):
        pltpu.make_async_copy(array, qo_v.at[i], loc.at[4]).start()

    load_x.wait()
    two = 2 * NX * octet
    with jax.named_scope("turn"):
        for i in range(NZH * NY // 2):
            turned = jnp.transpose(x_v[:, i * two : (i + 1) * two])
            xt[2 * i : 2 * i + 2] = turned.reshape(2, NX, octet, rows)

    with jax.named_scope("barrier_wait"):
        pl.semaphore_wait(barrier, len(partners))

    there = pl.ds(0, rows)

    def head_cols(c):
        return pl.ds(c * DH, DH)

    for c in range(heads):
        for i, src in enumerate((k_hbm, v_hbm)):
            remote(src.at[:, head_cols(c)], kv_v.at[i, there, head_cols(c)], kv_s.at[0], kv_r.at[c], (dp, after))

    def slots(d, count=1, e=0):
        return pl.ds((e * NX + d) * rows, count * rows)

    for d in (2, 3, 1):
        remote(xt.at[:, lax.rem(x + d, NX)], xr.at[:, :, slots(d)], x_s.at[0], x_r.at[d], in_x(d, 0))
    own_x = pltpu.make_async_copy(xt.at[:, x], xr.at[:, :, slots(0)], loc.at[5])
    own_x.start()

    load_order.wait()
    load_lens.wait()
    prior = before
    key_slots = [order[0, 2 * prior], order[0, 2 * prior + 1], order[0, 2 * ctx], order[0, 2 * ctx + 1]]
    bounds = [lens[0, 0]]
    for i in range(1, lens.shape[1] - 1):
        bounds.append(bounds[-1] + lens[0, i])

    def rank(pos):
        seg = jnp.zeros(pos.shape, jnp.int32)
        for bound in bounds:
            seg = seg + (pos >= bound).astype(jnp.int32)
        return seg

    shape = (2 * rows, rows)
    key_at = lax.broadcasted_iota(jnp.int32, shape, 0)
    query_at = lax.broadcasted_iota(jnp.int32, shape, 1)
    key_slot = jnp.where(
        key_at < rows,
        jnp.where(key_at < span, key_slots[0], key_slots[1]),
        jnp.where(key_at < rows + span, key_slots[2], key_slots[3]),
    )
    query_slot = jnp.where(query_at < span, key_slots[2], key_slots[3])
    key_pos = key_slot * span + key_at % span
    query_pos = query_slot * span + query_at % span
    allowed = (key_pos <= query_pos) & (rank(key_pos) == rank(query_pos))
    term = jnp.where(allowed, 0.0, -1e30).astype(F32)
    bias[...] = term

    own_x.wait()

    def hand(d):
        remote(xr.at[:, :, slots(d)], xr.at[:, :, slots(d, 1, 1)], hand_s.at[0], hand_r.at[0], in_x(0, 1))

    hand(0)
    wait(kv_v.at[:, here], loc.at[3])
    wait(qo_v, loc.at[4])

    def attend(c):
        keys, values = kv_v[0, :, head_cols(c)], kv_v[1, :, head_cols(c)]
        cols = [head_cols(c * shared + j) for j in range(shared)]
        query = jnp.concatenate([qo_v[0, :, col] for col in cols], axis=0)
        grad = jnp.concatenate([qo_v[1, :, col] for col in cols], axis=0)
        score = dot(keys, query, NT) + jnp.concatenate([bias[...]] * shared, axis=1)
        dprob = dot(values, grad, NT)
        top = jnp.max(score, axis=0, keepdims=True)
        expo = jnp.exp2((score - top) * (scale * math.log2(math.e)))
        prob = expo * (1.0 / jnp.sum(expo, axis=0, keepdims=True))
        prob_low = prob.astype(BF16)
        delta = jnp.sum(prob_low.astype(F32) * dprob, axis=0, keepdims=True)
        dscore = (prob * (dprob - delta)).astype(BF16)
        key_sum = dot(dscore, query, NN) * scale
        value_sum = dot(prob_low, grad, NN)
        back[c, 0] = key_sum[:rows].astype(BF16)
        back[c, 1] = value_sum[:rows].astype(BF16)
        remote(back.at[c], brecv.at[c], b_s.at[0], b_r.at[c], (dp, before))
        acc[c, 0] = key_sum[rows:]
        acc[c, 1] = value_sum[rows:]
        query_grad = (dot(dscore, keys, TN) * scale).astype(BF16)
        for j, col in enumerate(cols):
            qg_v[:, col] = query_grad[j * rows : (j + 1) * rows]

    for c in range(heads):
        with jax.named_scope("kv_wait"):
            wait(kv_v.at[:, there, head_cols(c)], kv_r.at[c])
        with jax.named_scope(f"attention{c}"):
            attend(c)
        cols = pl.ds(c * shared * DH, shared * DH)
        pltpu.make_async_copy(qg_v.at[:, cols], qg_out.at[:, cols], out_sem.at[0]).start()

    def finish(c):
        with jax.named_scope("back_wait"):
            wait(brecv.at[c], b_r.at[c])
        for t in range(2):
            kvg[c, t] = (acc[c, t] + brecv[c, t].astype(F32)).astype(BF16)
        for d, e in ((2, 0), (2, 1), (1, 0), (3, 0), (1, 1), (3, 1), (0, 1)):
            if d != 2 or c not in RELAYED:
                remote(kvg.at[c, lax.rem(core + e, NC)], gbuf.at[c, e * NX + d], g_s.at[0], g_r.at[c, int(d == 2)], in_x(d, e))
        gbuf[c, 0] = kvg[c, core]
        for t in range(2):
            pltpu.make_async_copy(kvg.at[c, t], kv_out.at[:, head_cols(t * heads + c)], out_sem.at[1]).start()

    with jax.named_scope("kv_grad0"):
        finish(0)
    with jax.named_scope("kv_grad1"):
        finish(1)
    with jax.named_scope("x_wait3"):
        wait(xr.at[:, :, slots(3)], x_r.at[3])
    hand(3)
    with jax.named_scope("kv_grad2"):
        finish(2)
    with jax.named_scope("kv_grad3"):
        finish(3)
    with jax.named_scope("x_wait1"):
        wait(xr.at[:, :, slots(1)], x_r.at[1])
    hand(1)
    with jax.named_scope("x_wait2"):
        wait(xr.at[:, :, slots(2)], x_r.at[2])
    hand(2)

    upper, lower = pl.ds(0, CUT), pl.ds(CUT, octet - CUT)

    def send_first(c, kind):
        def put(d, dst, last, to=None, part=pl.ds(0, octet)):
            remote(
                sent.at[c, kind, spot(kind, d), part], got.at[c, kind, dst, part], one_s.at[0],
                one_r.at[c, kind, last], rings[kind][1](d if to is None else to, 0),
            )

        if c in STEPS:
            put(4, 2, 0, -2, upper)
            put(4, 2, 0, 2, lower)
            put(-3, 0, 0, -1)
            put(3, 1, 0, 1)
            put(-1, 3, 1)
            put(1, 4, 1)
        else:
            for d in FAR:
                put(d, d - 1, 1)

    def combine(c, kind):
        with jax.named_scope("first_wait"):
            wait(got.at[c, kind, pl.ds(0, 3)], one_r.at[c, kind, 0])
        extra = got[c, kind, 2].astype(F32)
        row = lax.broadcasted_iota(jnp.int32, extra.shape, 0)
        for i, to in enumerate((-2, 2)):
            total = sent[c, kind, spot(kind, to)].astype(F32) + got[c, kind, i].astype(F32)
            mine = row < CUT if i == 0 else row >= CUT
            comb[c, kind, i] = (total + jnp.where(mine, extra, 0.0)).astype(BF16)
            remote(
                comb.at[c, kind, i], got.at[c, kind, 5 + i], one_s.at[0], one_r.at[c, kind, 1], rings[kind][1](to, 0)
            )

    def join(one, other):
        lane = lax.broadcasted_iota(jnp.int32, one.shape, 1)
        return jnp.where(lane < DH // 2, one, other)

    def swap(value):
        return pltpu.roll(value, DH // 2, 1)

    def multiply(c):
        with jax.named_scope("g_wait"):
            if c not in RELAYED:
                wait(gbuf.at[c, pl.ds(0, NX * NC - 3)], g_r.at[c, 0])
            wait(gbuf.at[c, pl.ds(0, NC)], g_r.at[c, 1])
        parts = [
            dot(
                xr[h * NY : (h + 1) * NY].reshape(NY * octet, NX * NC * rows),
                gbuf[c].reshape(NX * NC * rows, DH), NN,
            )
            for h in range(NZH)
        ]
        sent[c, 0] = join(parts[0], swap(parts[1])).astype(BF16).reshape(NY, octet, DH)
        send_first(c, 0)
        middle = NY * octet // 2
        for h in range(NZH):
            pf[h] = join(swap(parts[h][:middle]), parts[h][middle:])
            for i in range(NY // 2):
                for j in range(NZL):
                    zf[h * NZL + j, i * piece : (i + 1) * piece] = pf[
                        h, i * octet + j * piece : i * octet + (j + 1) * piece
                    ]
        sent[c, 1] = zf[...].astype(BF16)
        send_first(c, 1)

    def reduce(c, kind):
        first = 3 if c in STEPS else 0
        with jax.named_scope("last_wait"):
            wait(got.at[c, kind, pl.ds(first, NZ - 1 - first)], one_r.at[c, kind, 1])
        total = sent[c, kind, spot(kind, 0)].astype(F32)
        for i in range(first, NZ - 1):
            total = total + got[c, kind, i].astype(F32)
        tt[c, kind, :octet] = total

    def second(q, kind):
        one, other = tt[2 * q, kind], tt[2 * q + 1, kind]
        mm[0] = join(one, swap(other))
        mm[1] = join(swap(one), other)
        for h in range(2):
            for k in range(NZL * NC):
                s2[q, kind, h * NZL + k // NC, k % NC] = mm[h, k * own : k * own + PAD].astype(BF16)
        for d in FAR + (0,):
            for e in range(NC):
                if d or e:
                    remote(
                        s2.at[q, kind, spot(1 - kind, d), lax.rem(core + e, NC)], r2.at[q, kind, d * NC + e],
                        two_s.at[0], two_r.at[q, kind], rings[1 - kind][1](d, e),
                    )
        r2[q, kind, 0] = s2[q, kind, spot(1 - kind, 0), core]

    def total_of(q, kind):
        with jax.named_scope("second_wait"):
            wait(r2.at[q, kind, pl.ds(1, NY * NC - 1)], two_r.at[q, kind])
        sums = []
        for e in range(NC):
            total = r2[q, kind, e].astype(F32)
            for d in range(1, NY):
                total = total + r2[q, kind, d * NC + e].astype(F32)
            sums.append(total)
        return sums

    tt[:, :, octet:] = jnp.zeros((heads, 2, tt.shape[2] - octet, DH), F32)
    with jax.named_scope("hand_wait"):
        wait(xr.at[:, :, slots(0, NX, 1)], hand_r.at[0])

    def both(stage, c):
        with jax.named_scope(f"{stage.__name__}{c}"):
            stage(c, 0)
            stage(c, 1)

    with jax.named_scope("product0"):
        multiply(0)
    with jax.named_scope("product1"):
        multiply(1)
    with jax.named_scope("product2"):
        multiply(2)
    both(combine, 0)
    both(combine, 1)
    with jax.named_scope("product3"):
        multiply(3)
    both(combine, 2)
    both(reduce, 0)
    both(reduce, 1)
    both(second, 0)
    both(reduce, 2)
    both(reduce, 3)
    both(second, 1)

    with jax.named_scope("sends"):
        wait(kv_v.at[:, there], kv_s.at[0])
        wait(xr.at[:, :, slots(1, NX - 1)], x_s.at[0])
        wait(xr.at[:, :, slots(0, NX, 1)], hand_s.at[0])
        wait(brecv, b_s.at[0])
        wait(gbuf.at[:, pl.ds(1, NX * NC - 1)], g_s.at[0])
        wait(got, one_s.at[0])
        pltpu.make_async_copy(qg_v, qg_out, out_sem.at[0]).wait()
        wait(kv_out, out_sem.at[1])

    for q in range(heads // 2):
        one, other = total_of(q, 0), total_of(q, 1)
        for e in range(NC):
            for i, value in enumerate((join(one[e], swap(other[e])), join(swap(one[e]), other[e]))):
                col = ((lax.rem(core + e, NC)) * heads + 2 * q + i) * DH
                wv[:, pl.ds(pl.multiple_of(col, DH), DH)] = value[:own]
    with jax.named_scope("last"):
        copy = pltpu.make_async_copy(wv, w_out, out_sem.at[2])
        copy.start()
        wait(r2.at[:, :, pl.ds(1, NY * NC - 1)], two_s.at[0])
        copy.wait()


def place(qg_in, kv_in, w_in, qg_out, kv_out, w_out, qg, kv, w, got, put):
    rows = qg.shape[0] // 4
    plan = [(qg_in, qg_out, qg, pl.ds(i * rows, rows)) for i in range(4)]
    plan += [(kv_in, kv_out, kv, pl.ds(i * 2 * rows, 2 * rows)) for i in range(2)]
    plan += [(w_in, w_out, w, pl.ds(0, w.shape[0]))]
    loads = [pltpu.make_async_copy(a.at[r], v.at[r], got.at[i]) for i, (a, _, v, r) in enumerate(plan)]
    stores = [pltpu.make_async_copy(v.at[r], b.at[r], put.at[i]) for i, (_, b, v, r) in enumerate(plan)]
    for load in loads:
        load.start()
    for load, store in zip(loads, stores):
        load.wait()
        store.start()
    for store in stores:
        store.wait()


def body(queries, keys, values, out_grad, inputs, permutation, lengths):
    rows, model = inputs.shape
    heads = keys.shape[1] // DH
    own = model // (NZH * NY * NX * NZL * NC)
    octet = NZL * NC * own
    room = -(-(octet - own + PAD) // 8) * 8
    vmem = lambda kind, *shape: pltpu.VMEM(shape, kind)
    dma = lambda *shape: pltpu.SemaphoreType.DMA(shape)
    scratch = [
        pltpu.SMEM(permutation.shape, jnp.int32),
        pltpu.SMEM(lengths.shape, jnp.int32),
        vmem(BF16, rows, model),
        vmem(BF16, 2, *queries.shape),
        vmem(BF16, 2, 2 * rows, heads * DH),
        vmem(F32, 2 * rows, rows),
        vmem(BF16, *queries.shape),
        vmem(F32, heads, 2, rows, DH),
        vmem(BF16, heads, 2, rows, DH),
        vmem(BF16, heads, 2, rows, DH),
        vmem(BF16, heads, 2, rows, DH),
        vmem(BF16, heads, NX * NC, rows, DH),
        vmem(BF16, NZH * NY, NX, octet, rows),
        vmem(BF16, NZH * NY, octet, NX * NC * rows),
        vmem(F32, NZH, NY * octet // 2, DH),
        vmem(F32, NZ, octet, DH),
        vmem(BF16, heads, 2, NY, octet, DH),
        vmem(BF16, heads, 2, 2, octet, DH),
        vmem(BF16, heads, 2, NY - 1, octet, DH),
        vmem(F32, heads, 2, room, DH),
        vmem(F32, 2, room, DH),
        vmem(BF16, heads // 2, 2, NY, NC, PAD, DH),
        vmem(BF16, heads // 2, 2, NY * NC, PAD, DH),
        vmem(F32, own, 2 * heads * DH),
        dma(6), dma(3),
        dma(1), dma(heads),
        dma(1), dma(NX), dma(1), dma(1),
        dma(1), dma(heads),
        dma(1), dma(heads, 2),
        dma(1), dma(heads, 2, 2),
        dma(1), dma(heads // 2, 2),
    ]
    anywhere = pl.BlockSpec(memory_space=pl.ANY)
    shapes = (
        jax.ShapeDtypeStruct(queries.shape, BF16),
        jax.ShapeDtypeStruct((rows, 2 * heads * DH), BF16),
        jax.ShapeDtypeStruct((own, 2 * heads * DH), F32),
    )
    results = pl.pallas_call(
        kernel,
        out_shape=shapes,
        in_specs=[anywhere] * 7,
        out_specs=(anywhere,) * 3,
        scratch_shapes=scratch,
        compiler_params=pltpu.CompilerParams(
            collective_id=0, has_side_effects=True, vmem_limit_bytes=63 * 1024 * 1024
        ),
    )(permutation, lengths, queries, keys, values, out_grad, inputs)
    return pl.pallas_call(
        place,
        out_shape=shapes,
        in_specs=[anywhere] * 3,
        out_specs=(anywhere,) * 3,
        scratch_shapes=[vmem(r.dtype, *r.shape) for r in shapes] + [dma(7), dma(7)],
        compiler_params=pltpu.CompilerParams(vmem_limit_bytes=63 * 1024 * 1024),
    )(*results)


def solution(mesh):
    both = P(("dp", "ctx"), None)
    return jax.shard_map(
        body,
        mesh=mesh,
        in_specs=(both, both, both, both, both, P("dp", None), P("dp", None)),
        out_specs=(both, both, both),
        check_vma=False,
    )
```

```python
import functools
import math

import jax
import jax.numpy as jnp
from jax import lax
from jax.experimental import pallas as pl
from jax.experimental.pallas import tpu as pltpu
from jax.sharding import PartitionSpec as P

DH = 128
NZH, NY, NX, NZL, NC = 2, 8, 4, 4, 2
NZ = NZH * NZL
PAD = 16
FAR = (4, 3, 5, 2, 6, 1, 7)
RELAYED = ()
CUT = 48
STEPS = (0, 1, 2)
MESH = pl.DeviceIdType.MESH
F32, BF16 = jnp.float32, jnp.bfloat16
NT = (((1,), (1,)), ((), ()))
NN = (((1,), (0,)), ((), ()))
TN = (((0,), (0,)), ((), ()))


def dot(a, b, dims):
    return lax.dot_general(a, b, dims, preferred_element_type=F32)


def kernel(
    order_hbm, lens_hbm, q_hbm, k_hbm, v_hbm, og_hbm, x_hbm, qg_out, kv_out, w_out,
    order, lens, x_v, qo_v, kv_v, bias, qg_v, acc, back, brecv, kvg, gbuf, xt, xr,
    pf, zf, sent, comb, got, tt, mm, s2, r2, wv,
    loc, out_sem, kv_s, kv_r, x_s, x_r, hand_s, hand_r, b_s, b_r, g_s, g_r, one_s, one_r, two_s, two_r,
):
    rows = k_hbm.shape[0]
    span = rows // 2
    heads = k_hbm.shape[1] // DH
    shared = q_hbm.shape[1] // (DH * heads)
    own = w_out.shape[0]
    octet = NZL * NC * own
    piece = NC * own
    scale = 1.0 / DH**0.5

    dp, ctx = lax.axis_index("dp"), lax.axis_index("ctx")
    cycle = NX * NZL * NC
    zhi, y = lax.div(dp, NY), lax.rem(dp, NY)
    x, zlo, core = lax.div(ctx, NZL * NC), lax.rem(lax.div(ctx, NC), NZL), lax.rem(ctx, NC)
    z = zhi * NZL + zlo
    after, before = lax.rem(ctx + 1, cycle), lax.rem(ctx + cycle - 1, cycle)

    def device(x, y, z, e):
        return (lax.div(z, NZL) * NY + y, x * (NZL * NC) + lax.rem(z, NZL) * NC + (lax.rem(core + e, NC) if e else core))

    def in_x(d, e):
        return device(lax.rem(x + d, NX), y, z, e)

    def in_y(d, e):
        return device(x, lax.rem(y + NY + d, NY), z, e)

    def in_z(d, e):
        return device(x, y, lax.rem(z + NZ + d, NZ), e)

    rings = ((y, in_y), (z, in_z))

    def spot(kind, d):
        return lax.rem(rings[kind][0] + NZ + d, NZ)

    def remote(src, dst, send, recv, to):
        copy = pltpu.make_async_remote_copy(
            src_ref=src, dst_ref=dst, send_sem=send, recv_sem=recv, device_id=to, device_id_type=MESH
        )
        copy.start()

    def wait(array, sem):
        pltpu.make_async_copy(array, array, sem).wait()

    partners = [(dp, after), (dp, before)]
    partners += [where(d, e) for d in FAR for _, where in rings for e in range(NC)]
    partners += [in_x(d, e) for d in range(NX) for e in range(NC) if d or e]
    barrier = pltpu.get_barrier_semaphore()
    load_x = pltpu.make_async_copy(x_hbm, x_v, loc.at[0])
    load_x.start()
    for to in partners:
        pl.semaphore_signal(barrier, inc=1, device_id=to, device_id_type=MESH)

    here = pl.ds(rows, rows)
    load_order = pltpu.make_async_copy(order_hbm, order, loc.at[1])
    load_lens = pltpu.make_async_copy(lens_hbm, lens, loc.at[2])
    load_order.start()
    load_lens.start()
    for i, array in enumerate((k_hbm, v_hbm)):
        pltpu.make_async_copy(array, kv_v.at[i, here], loc.at[3]).start()
    for i, array in enumerate((q_hbm, og_hbm)):
        pltpu.make_async_copy(array, qo_v.at[i], loc.at[4]).start()

    load_x.wait()
    two = 2 * NX * octet
    with jax.named_scope("turn"):
        for i in range(NZH * NY // 2):
            turned = jnp.transpose(x_v[:, i * two : (i + 1) * two])
            xt[2 * i : 2 * i + 2] = turned.reshape(2, NX, octet, rows)

    with jax.named_scope("barrier_wait"):
        pl.semaphore_wait(barrier, len(partners))

    there = pl.ds(0, rows)

    def head_cols(c):
        return pl.ds(c * DH, DH)

    for c in range(heads):
        for i, src in enumerate((k_hbm, v_hbm)):
            remote(src.at[:, head_cols(c)], kv_v.at[i, there, head_cols(c)], kv_s.at[0], kv_r.at[c], (dp, after))

    def slots(d, count=1, e=0):
        return pl.ds((e * NX + d) * rows, count * rows)

    def blocks(h):
        return pl.ds(h * NY, NY)

    for h in range(NZH):
        for d in (2, 3, 1):
            remote(
                xt.at[blocks(h), lax.rem(x + d, NX)], xr.at[blocks(h), :, slots(d)], x_s.at[0], x_r.at[h], in_x(d, 0)
            )
    own_x = pltpu.make_async_copy(xt.at[:, x], xr.at[:, :, slots(0)], loc.at[5])
    own_x.start()

    load_order.wait()
    load_lens.wait()
    prior = before
    key_slots = [order[0, 2 * prior], order[0, 2 * prior + 1], order[0, 2 * ctx], order[0, 2 * ctx + 1]]
    bounds = [lens[0, 0]]
    for i in range(1, lens.shape[1] - 1):
        bounds.append(bounds[-1] + lens[0, i])

    def rank(pos):
        seg = jnp.zeros(pos.shape, jnp.int32)
        for bound in bounds:
            seg = seg + (pos >= bound).astype(jnp.int32)
        return seg

    shape = (2 * rows, rows)
    key_at = lax.broadcasted_iota(jnp.int32, shape, 0)
    query_at = lax.broadcasted_iota(jnp.int32, shape, 1)
    key_slot = jnp.where(
        key_at < rows,
        jnp.where(key_at < span, key_slots[0], key_slots[1]),
        jnp.where(key_at < rows + span, key_slots[2], key_slots[3]),
    )
    query_slot = jnp.where(query_at < span, key_slots[2], key_slots[3])
    key_pos = key_slot * span + key_at % span
    query_pos = query_slot * span + query_at % span
    allowed = (key_pos <= query_pos) & (rank(key_pos) == rank(query_pos))
    term = jnp.where(allowed, 0.0, -1e30).astype(F32)
    bias[...] = term

    own_x.wait()

    def hand(h, d, count):
        remote(
            xr.at[blocks(h), :, slots(d, count)], xr.at[blocks(h), :, slots(d, count, 1)],
            hand_s.at[0], hand_r.at[0], in_x(0, 1),
        )

    for h in range(NZH):
        hand(h, 0, 1)
    wait(kv_v.at[:, here], loc.at[3])
    wait(qo_v, loc.at[4])

    def attend(c):
        keys, values = kv_v[0, :, head_cols(c)], kv_v[1, :, head_cols(c)]
        cols = [head_cols(c * shared + j) for j in range(shared)]
        query = jnp.concatenate([qo_v[0, :, col] for col in cols], axis=0)
        grad = jnp.concatenate([qo_v[1, :, col] for col in cols], axis=0)
        score = dot(keys, query, NT) + jnp.concatenate([bias[...]] * shared, axis=1)
        dprob = dot(values, grad, NT)
        top = jnp.max(score, axis=0, keepdims=True)
        expo = jnp.exp2((score - top) * (scale * math.log2(math.e)))
        prob = expo * (1.0 / jnp.sum(expo, axis=0, keepdims=True))
        prob_low = prob.astype(BF16)
        delta = jnp.sum(prob_low.astype(F32) * dprob, axis=0, keepdims=True)
        dscore = (prob * (dprob - delta)).astype(BF16)
        key_sum = dot(dscore, query, NN) * scale
        value_sum = dot(prob_low, grad, NN)
        back[c, 0] = key_sum[:rows].astype(BF16)
        back[c, 1] = value_sum[:rows].astype(BF16)
        remote(back.at[c], brecv.at[c], b_s.at[0], b_r.at[c], (dp, before))
        acc[c, 0] = key_sum[rows:]
        acc[c, 1] = value_sum[rows:]
        query_grad = (dot(dscore, keys, TN) * scale).astype(BF16)
        for j, col in enumerate(cols):
            qg_v[:, col] = query_grad[j * rows : (j + 1) * rows]

    for c in range(heads):
        with jax.named_scope("kv_wait"):
            wait(kv_v.at[:, there, head_cols(c)], kv_r.at[c])
        with jax.named_scope(f"attention{c}"):
            attend(c)
        cols = pl.ds(c * shared * DH, shared * DH)
        pltpu.make_async_copy(qg_v.at[:, cols], qg_out.at[:, cols], out_sem.at[0]).start()

    def finish(c):
        with jax.named_scope("back_wait"):
            wait(brecv.at[c], b_r.at[c])
        for t in range(2):
            kvg[c, t] = (acc[c, t] + brecv[c, t].astype(F32)).astype(BF16)
        for d, e in ((2, 0), (2, 1), (1, 0), (3, 0), (1, 1), (3, 1), (0, 1)):
            if d != 2 or c not in RELAYED:
                remote(kvg.at[c, lax.rem(core + e, NC)], gbuf.at[c, e * NX + d], g_s.at[0], g_r.at[c, int(d == 2)], in_x(d, e))
        gbuf[c, 0] = kvg[c, core]
        for t in range(2):
            pltpu.make_async_copy(kvg.at[c, t], kv_out.at[:, head_cols(t * heads + c)], out_sem.at[1]).start()

    with jax.named_scope("kv_grad0"):
        finish(0)
    with jax.named_scope("kv_grad1"):
        finish(1)
    with jax.named_scope("x_wait0"):
        wait(xr.at[blocks(0), :, slots(1, NX - 1)], x_r.at[0])
    hand(0, 1, NX - 1)
    with jax.named_scope("kv_grad2"):
        finish(2)
    with jax.named_scope("kv_grad3"):
        finish(3)
    with jax.named_scope("x_wait1"):
        wait(xr.at[blocks(1), :, slots(1, NX - 1)], x_r.at[1])
    hand(1, 1, NX - 1)

    upper, lower = pl.ds(0, CUT), pl.ds(CUT, octet - CUT)

    def send_first(c, kind):
        def put(d, dst, last, to=None, part=pl.ds(0, octet)):
            remote(
                sent.at[c, kind, spot(kind, d), part], got.at[c, kind, dst, part], one_s.at[0],
                one_r.at[c, kind, last], rings[kind][1](d if to is None else to, 0),
            )

        if c in STEPS:
            put(4, 2, 0, -2, upper)
            put(4, 2, 0, 2, lower)
            put(-3, 0, 0, -1)
            put(3, 1, 0, 1)
            put(-1, 3, 1)
            put(1, 4, 1)
        else:
            for d in FAR:
                put(d, d - 1, 1)

    def combine(c, kind):
        with jax.named_scope("first_wait"):
            wait(got.at[c, kind, pl.ds(0, 3)], one_r.at[c, kind, 0])
        extra = got[c, kind, 2].astype(F32)
        row = lax.broadcasted_iota(jnp.int32, extra.shape, 0)
        for i, to in enumerate((-2, 2)):
            total = sent[c, kind, spot(kind, to)].astype(F32) + got[c, kind, i].astype(F32)
            mine = row < CUT if i == 0 else row >= CUT
            comb[c, kind, i] = (total + jnp.where(mine, extra, 0.0)).astype(BF16)
            remote(
                comb.at[c, kind, i], got.at[c, kind, 5 + i], one_s.at[0], one_r.at[c, kind, 1], rings[kind][1](to, 0)
            )

    def join(one, other):
        lane = lax.broadcasted_iota(jnp.int32, one.shape, 1)
        return jnp.where(lane < DH // 2, one, other)

    def swap(value):
        return pltpu.roll(value, DH // 2, 1)

    def multiply(c):
        with jax.named_scope("g_wait"):
            if c not in RELAYED:
                wait(gbuf.at[c, pl.ds(0, NX * NC - 3)], g_r.at[c, 0])
            wait(gbuf.at[c, pl.ds(0, NC)], g_r.at[c, 1])
        parts = [
            dot(
                xr[h * NY : (h + 1) * NY].reshape(NY * octet, NX * NC * rows),
                gbuf[c].reshape(NX * NC * rows, DH), NN,
            )
            for h in range(NZH)
        ]
        sent[c, 0] = join(parts[0], swap(parts[1])).astype(BF16).reshape(NY, octet, DH)
        send_first(c, 0)
        middle = NY * octet // 2
        for h in range(NZH):
            pf[h] = join(swap(parts[h][:middle]), parts[h][middle:])
            for i in range(NY // 2):
                for j in range(NZL):
                    zf[h * NZL + j, i * piece : (i + 1) * piece] = pf[
                        h, i * octet + j * piece : i * octet + (j + 1) * piece
                    ]
        sent[c, 1] = zf[...].astype(BF16)
        send_first(c, 1)

    def reduce(c, kind):
        first = 3 if c in STEPS else 0
        with jax.named_scope("last_wait"):
            wait(got.at[c, kind, pl.ds(first, NZ - 1 - first)], one_r.at[c, kind, 1])
        total = sent[c, kind, spot(kind, 0)].astype(F32)
        for i in range(first, NZ - 1):
            total = total + got[c, kind, i].astype(F32)
        tt[c, kind, :octet] = total

    def second(q, kind):
        one, other = tt[2 * q, kind], tt[2 * q + 1, kind]
        mm[0] = join(one, swap(other))
        mm[1] = join(swap(one), other)
        for h in range(2):
            for k in range(NZL * NC):
                s2[q, kind, h * NZL + k // NC, k % NC] = mm[h, k * own : k * own + PAD].astype(BF16)
        for d in FAR + (0,):
            for e in range(NC):
                if d or e:
                    remote(
                        s2.at[q, kind, spot(1 - kind, d), lax.rem(core + e, NC)], r2.at[q, kind, d * NC + e],
                        two_s.at[0], two_r.at[q, kind], rings[1 - kind][1](d, e),
                    )
        r2[q, kind, 0] = s2[q, kind, spot(1 - kind, 0), core]

    def total_of(q, kind):
        with jax.named_scope("second_wait"):
            wait(r2.at[q, kind, pl.ds(1, NY * NC - 1)], two_r.at[q, kind])
        sums = []
        for e in range(NC):
            total = r2[q, kind, e].astype(F32)
            for d in range(1, NY):
                total = total + r2[q, kind, d * NC + e].astype(F32)
            sums.append(total)
        return sums

    tt[:, :, octet:] = jnp.zeros((heads, 2, tt.shape[2] - octet, DH), F32)
    with jax.named_scope("hand_wait"):
        wait(xr.at[:, :, slots(0, NX, 1)], hand_r.at[0])

    def both(stage, c):
        with jax.named_scope(f"{stage.__name__}{c}"):
            stage(c, 0)
            stage(c, 1)

    with jax.named_scope("product0"):
        multiply(0)
    with jax.named_scope("product1"):
        multiply(1)
    with jax.named_scope("product2"):
        multiply(2)
    both(combine, 0)
    both(combine, 1)
    with jax.named_scope("product3"):
        multiply(3)
    both(combine, 2)
    both(reduce, 0)
    both(reduce, 1)
    both(second, 0)
    both(reduce, 2)
    both(reduce, 3)
    both(second, 1)

    with jax.named_scope("sends"):
        wait(kv_v.at[:, there], kv_s.at[0])
        wait(xr.at[:, :, slots(1, NX - 1)], x_s.at[0])
        wait(xr.at[:, :, slots(0, NX, 1)], hand_s.at[0])
        wait(brecv, b_s.at[0])
        wait(gbuf.at[:, pl.ds(1, NX * NC - 1)], g_s.at[0])
        wait(got, one_s.at[0])
        pltpu.make_async_copy(qg_v, qg_out, out_sem.at[0]).wait()
        wait(kv_out, out_sem.at[1])

    for q in range(heads // 2):
        one, other = total_of(q, 0), total_of(q, 1)
        for e in range(NC):
            for i, value in enumerate((join(one[e], swap(other[e])), join(swap(one[e]), other[e]))):
                col = ((lax.rem(core + e, NC)) * heads + 2 * q + i) * DH
                wv[:, pl.ds(pl.multiple_of(col, DH), DH)] = value[:own]
    with jax.named_scope("last"):
        copy = pltpu.make_async_copy(wv, w_out, out_sem.at[2])
        copy.start()
        wait(r2.at[:, :, pl.ds(1, NY * NC - 1)], two_s.at[0])
        copy.wait()


def place(qg_in, kv_in, w_in, qg_out, kv_out, w_out, qg, kv, w, got, put):
    rows = qg.shape[0] // 4
    plan = [(qg_in, qg_out, qg, pl.ds(i * rows, rows)) for i in range(4)]
    plan += [(kv_in, kv_out, kv, pl.ds(i * 2 * rows, 2 * rows)) for i in range(2)]
    plan += [(w_in, w_out, w, pl.ds(0, w.shape[0]))]
    loads = [pltpu.make_async_copy(a.at[r], v.at[r], got.at[i]) for i, (a, _, v, r) in enumerate(plan)]
    stores = [pltpu.make_async_copy(v.at[r], b.at[r], put.at[i]) for i, (_, b, v, r) in enumerate(plan)]
    for load in loads:
        load.start()
    for load, store in zip(loads, stores):
        load.wait()
        store.start()
    for store in stores:
        store.wait()


def body(queries, keys, values, out_grad, inputs, permutation, lengths):
    rows, model = inputs.shape
    heads = keys.shape[1] // DH
    own = model // (NZH * NY * NX * NZL * NC)
    octet = NZL * NC * own
    room = -(-(octet - own + PAD) // 8) * 8
    vmem = lambda kind, *shape: pltpu.VMEM(shape, kind)
    dma = lambda *shape: pltpu.SemaphoreType.DMA(shape)
    scratch = [
        pltpu.SMEM(permutation.shape, jnp.int32),
        pltpu.SMEM(lengths.shape, jnp.int32),
        vmem(BF16, rows, model),
        vmem(BF16, 2, *queries.shape),
        vmem(BF16, 2, 2 * rows, heads * DH),
        vmem(F32, 2 * rows, rows),
        vmem(BF16, *queries.shape),
        vmem(F32, heads, 2, rows, DH),
        vmem(BF16, heads, 2, rows, DH),
        vmem(BF16, heads, 2, rows, DH),
        vmem(BF16, heads, 2, rows, DH),
        vmem(BF16, heads, NX * NC, rows, DH),
        vmem(BF16, NZH * NY, NX, octet, rows),
        vmem(BF16, NZH * NY, octet, NX * NC * rows),
        vmem(F32, NZH, NY * octet // 2, DH),
        vmem(F32, NZ, octet, DH),
        vmem(BF16, heads, 2, NY, octet, DH),
        vmem(BF16, heads, 2, 2, octet, DH),
        vmem(BF16, heads, 2, NY - 1, octet, DH),
        vmem(F32, heads, 2, room, DH),
        vmem(F32, 2, room, DH),
        vmem(BF16, heads // 2, 2, NY, NC, PAD, DH),
        vmem(BF16, heads // 2, 2, NY * NC, PAD, DH),
        vmem(F32, own, 2 * heads * DH),
        dma(6), dma(3),
        dma(1), dma(heads),
        dma(1), dma(NZH), dma(1), dma(1),
        dma(1), dma(heads),
        dma(1), dma(heads, 2),
        dma(1), dma(heads, 2, 2),
        dma(1), dma(heads // 2, 2),
    ]
    anywhere = pl.BlockSpec(memory_space=pl.ANY)
    shapes = (
        jax.ShapeDtypeStruct(queries.shape, BF16),
        jax.ShapeDtypeStruct((rows, 2 * heads * DH), BF16),
        jax.ShapeDtypeStruct((own, 2 * heads * DH), F32),
    )
    results = pl.pallas_call(
        kernel,
        out_shape=shapes,
        in_specs=[anywhere] * 7,
        out_specs=(anywhere,) * 3,
        scratch_shapes=scratch,
        compiler_params=pltpu.CompilerParams(
            collective_id=0, has_side_effects=True, vmem_limit_bytes=63 * 1024 * 1024
        ),
    )(permutation, lengths, queries, keys, values, out_grad, inputs)
    return pl.pallas_call(
        place,
        out_shape=shapes,
        in_specs=[anywhere] * 3,
        out_specs=(anywhere,) * 3,
        scratch_shapes=[vmem(r.dtype, *r.shape) for r in shapes] + [dma(7), dma(7)],
        compiler_params=pltpu.CompilerParams(vmem_limit_bytes=63 * 1024 * 1024),
    )(*results)


def solution(mesh):
    both = P(("dp", "ctx"), None)
    return jax.shard_map(
        body,
        mesh=mesh,
        in_specs=(both, both, both, both, both, P("dp", None), P("dp", None)),
        out_specs=(both, both, both),
        check_vma=False,
    )
```
